32 devices in a mesh: shot: 16 (over z, y, core), tm: 2 (over x).
Axes of the slice: x: 2, y: 2, z: 4, core: 2. Of those that a mesh axis runs over, the one named last changes fastest.
Arguments:
- records: bfloat16 [16, 4, 32, 256], P('shot', None, None, 'tm'), may hold values from -6 to 6
- fan_taps: bfloat16 [4, 15, 15], replicated, may hold values from -0.29882812 to 0.29882812
- dip_taps: bfloat16 [15, 15], replicated, may hold values from -0.29882812 to 0.29882812
- live_mask: int32 [16, 32], P('shot'), may hold values from 0 to 1, as said below
- node_place: int32 [32], replicated, may hold values from 0 to 31, as said below
- shot_place: int32 [16], replicated, may hold values from 0 to 15, as said below
Outputs:
- node_gathers: bfloat16 [16, 4, 32, 256], P(None, None, 'shot', 'tm')
The draws below stay inside these ranges and needn't reach their ends.
Inputs may be any that keep to these rules, and one draw needn't show every extreme that they name: `live_mask`: A trace is live only where the node lies within 16 positions of the shot's point on the receiver line; some traces inside that band are dead too. `node_place`: A permutation: every position once. `shot_place`: A permutation: every position once.
All inputs are finite; a program needn't handle non-finite values.
Results may differ from the reference program's by a relative error of at most 0.0049.
Values may be sent and summed in bfloat16 or wider, within the bound.
A program may use at most 64 MiB of HBM per device.

```python
import jax
import jax.numpy as jnp
from jax import lax

C = 4
TAPS = 15
SHOTS = 16
NODES = 32
TIME = 256


def geometry(key):
    node_place = jax.random.permutation(jax.random.fold_in(key, 101), NODES).astype(jnp.int32)
    shot_place = jax.random.permutation(jax.random.fold_in(key, 102), SHOTS).astype(jnp.int32)
    source_spot = shot_place * NODES // SHOTS
    offset = jnp.abs(source_spot[:, None] - node_place[None, :])
    recorded = jax.random.randint(jax.random.fold_in(key, 103), (SHOTS, NODES), 0, 16)
    live_mask = jnp.where((offset <= NODES // 2) & (recorded != 0), 1, 0).astype(jnp.int32)
    return (node_place, shot_place, live_mask)


def draw_live_mask(key, part):
    return geometry(key)[2]


def draw_node_place(key, part):
    return geometry(key)[0]


def draw_shot_place(key, part):
    return geometry(key)[1]


def steps_of(key, shape, shards, smallest, largest):
    loudness, own = 1.0, jax.random.fold_in(key, 6)
    for position, parts in shards:
        steps = jnp.exp(jax.random.uniform(jax.random.fold_in(own, position), (parts,), jnp.float32, smallest / len(shards), largest / len(shards)))
        loudness = loudness * jnp.repeat(steps, shape[position] // parts).reshape([-1 if axis == position else 1 for axis in range(len(shape))])
    return loudness


def bell_draw(own_key, shape, scale, reach, split=(), dtype=jnp.bfloat16):
    entries = scale * jax.random.normal(own_key, shape, jnp.float32)
    if split:
        entries = entries * steps_of(own_key, shape, split, -0.22, 0.18)
    return jnp.clip(entries, -reach, reach).astype(dtype)


def setup_inputs(seed: int = 0) -> dict:
    splits = jax.random.split(jax.random.key(seed), 7)
    return {
        "records": bell_draw(splits[0], (SHOTS, C, NODES, TIME), 1.0, 6.0, ((0, 16), (3, 2))),
        "fan_taps": bell_draw(splits[1], (C, TAPS, TAPS), 0.0667, 0.29882812),
        "dip_taps": bell_draw(splits[2], (TAPS, TAPS), 0.0667, 0.29882812),
        "live_mask": draw_live_mask(jax.random.fold_in(splits[6], 71), 0),
        "node_place": draw_node_place(jax.random.fold_in(splits[6], 71), 0),
        "shot_place": draw_shot_place(jax.random.fold_in(splits[6], 71), 0),
    }


def fan_block(block_data, fan_kernel):
    half = (TAPS - 1) // 2
    return lax.conv_general_dilated(block_data.astype(jnp.float32), fan_kernel, window_strides=(1, 1), padding=((half, half), (half, half)), dimension_numbers=("NCHW", "OIHW", "NCHW"), feature_group_count=C, precision=lax.Precision.HIGHEST)


def dip_block(block_data, dip_kernel):
    half = (TAPS - 1) // 2
    return lax.conv_general_dilated(block_data.astype(jnp.float32), dip_kernel, window_strides=(1, 1), padding=((half, half), (half, half)), dimension_numbers=("NCHW", "OIHW", "NCHW"), precision=lax.Precision.HIGHEST)


def reference(records, fan_taps, dip_taps, live_mask, node_place, shot_place):
    node_order = jnp.argsort(node_place).astype(jnp.int32)
    shot_order = jnp.argsort(shot_place).astype(jnp.int32)
    ordered = jnp.take(records, node_order, axis=2)
    fan_kernel = fan_taps.astype(jnp.float32)[:, None]
    blocks = ordered.reshape(SHOTS // 8, 8, C, NODES, TIME)
    fan_field = lax.map(lambda block_data: fan_block(block_data, fan_kernel), blocks).reshape(SHOTS, C, NODES, TIME)
    live_sorted = jnp.take(live_mask, node_order, axis=1).astype(jnp.float32)
    fanned = (fan_field * live_sorted[:, None, :, None]).astype(jnp.bfloat16)
    gathered = jnp.take(fanned, shot_order, axis=0)
    node_lines = gathered.transpose(1, 2, 0, 3).reshape(C * NODES // 8, 8, 1, SHOTS, TIME)
    dip_kernel = dip_taps.astype(jnp.float32)[None, None]
    filtered = lax.map(lambda block_data: dip_block(block_data, dip_kernel), node_lines)
    filtered = filtered.reshape(C, NODES, SHOTS, TIME).transpose(2, 0, 1, 3)
    return filtered.astype(jnp.bfloat16)
```

```python
import functools

import jax
import jax.numpy as jnp
from jax import lax
from jax.experimental import pallas as pl
from jax.experimental.pallas import tpu as pltpu
from jax.sharding import PartitionSpec as P

MESH = pl.DeviceIdType.MESH


def repeat(count, body):
    if count <= 32:
        for step in range(count):
            body(step)
    else:
        lax.fori_loop(0, count, lambda step, carry: (body(step), carry)[1], 0)


def spread_taps(taps, groups, width):
    first = lax.broadcasted_iota(jnp.int32, (taps.shape[1], width), 0) * groups
    lane = lax.broadcasted_iota(jnp.int32, (taps.shape[1], width), 1)
    onehot = jnp.where((lane >= first) & (lane < first + groups), 1.0, 0.0).astype(jnp.bfloat16)
    return jnp.dot(taps, onehot, preferred_element_type=jnp.float32)


def spread_places(place, groups, width):
    row = lax.broadcasted_iota(jnp.int32, (groups, width), 0)
    lane = lax.broadcasted_iota(jnp.int32, (groups, width), 1)
    onehot = jnp.where(lax.rem(lane, groups) == row, 1.0, 0.0).astype(jnp.bfloat16)
    left = jnp.broadcast_to(place.astype(jnp.float32), (8, groups)).astype(jnp.bfloat16)
    return jnp.dot(left, onehot, preferred_element_type=jnp.float32).astype(jnp.int32)


def kernel(
    records_ref, fan_ref, dip_ref, live_ref, node_ref, shot_ref, out_ref,
    traces, matrix, shifted, framed, send, recv, flat, rows, pack, from_low, from_high,
    load_sem, send_sem, recv_sem, pack_sem, low_sem, high_sem,
):
    comps, nodes, samples = traces.shape
    devices = send.shape[0]
    each = nodes // devices
    groups = comps * each
    tap_count = dip_ref.shape[0]
    reach = (tap_count - 1) // 2
    me, win = lax.axis_index("shot"), lax.axis_index("tm")
    windows = lax.axis_size("tm")
    has_low, has_high = win > 0, win < windows - 1

    load = pltpu.make_async_copy(records_ref.at[0], traces, load_sem)
    load.start()

    barrier = pltpu.get_barrier_semaphore()

    def greet(step):
        pl.semaphore_signal(
            barrier, inc=1, device_id=(lax.rem(me + step + 1, devices), win), device_id_type=MESH
        )

    repeat(devices - 1, greet)
    for there, side in ((has_low, -1), (has_high, 1)):
        @pl.when(there)
        def _():
            repeat(devices, lambda step: pl.semaphore_signal(
                barrier, inc=1, device_id=(lax.rem(me + step, devices), win + side),
                device_id_type=MESH,
            ))

    depth = matrix.shape[2]
    taps = [spread_taps(fan_ref[c], nodes, depth) for c in range(comps)]
    places = spread_places(node_ref[...], nodes, depth)[0:1]
    block = min(devices, 16)

    def build(step):
        for j in range(each):
            at = (lax.broadcasted_iota(jnp.int32, (block, depth), 0) + step * block) * each + j
            apart = places - at + reach
            sums = [jnp.zeros((block, depth), jnp.float32)] * comps
            for a in range(tap_count):
                hit = apart == a
                sums = [jnp.where(hit, taps[c][a : a + 1], sums[c]) for c in range(comps)]
            for c in range(comps):
                start = j * devices + step * block
                if not isinstance(step, int):
                    start = pl.multiple_of(start, block)
                matrix[c, pl.ds(start, block), :] = sums[c].astype(jnp.bfloat16)

    if devices == block:
        build(0)
    else:
        lax.fori_loop(0, devices // block, lambda step, carry: (build(step), carry)[1], 0)

    position = lax.broadcasted_iota(jnp.int32, (devices, nodes), 0) * each
    alive = []
    for j in range(each):
        here = node_ref[...] == position + j
        kept = jnp.where(here, live_ref[...].astype(jnp.float32), 0.0)
        alive.append(jnp.sum(kept, axis=1, keepdims=True))

    load.wait()
    lane = lax.broadcasted_iota(jnp.int32, (nodes, samples), 1)
    for c in range(comps):
        trace = traces[c].astype(jnp.float32)
        for b in range(tap_count):
            move = b - reach
            turned = pltpu.roll(trace, (-move) % samples, 1) if move else trace
            inside = (lane < samples - move) if move >= 0 else (lane >= -move)
            shifted[c, b * nodes : (b + 1) * nodes, :samples] = (
                jnp.where(inside, turned, 0.0).astype(jnp.bfloat16)
            )
            shifted[c, b * nodes : (b + 1) * nodes, samples:] = (
                jnp.where(inside, 0.0, turned).astype(jnp.bfloat16)
            )
        rest = depth - tap_count * nodes
        shifted[c, tap_count * nodes :, :] = jnp.zeros((rest, 2 * samples), jnp.bfloat16)

    lane = lax.broadcasted_iota(jnp.int32, (devices, samples), 1)
    stride = samples // groups
    to_low = jnp.zeros((devices, samples), jnp.float32)
    to_high = jnp.zeros((devices, samples), jnp.float32)
    for c in range(comps):
        field = jnp.dot(matrix[c], shifted[c], preferred_element_type=jnp.float32)
        for j in range(each):
            g = c * each + j
            part = field[j * devices : (j + 1) * devices] * alive[j]
            inner, outer = part[:, :samples], part[:, samples:]
            flat[pl.ds(g, devices, stride=2 * groups), :] = inner
            flat[pl.ds(groups + g, devices, stride=2 * groups), :] = outer
            mine = (lane >= g * stride) & (lane < g * stride + 2 * reach)
            turn = (reach + g * stride) % samples
            low = jnp.where(lane >= samples // 2, outer, inner)
            high = jnp.where(lane >= samples // 2, inner, outer)
            to_low = jnp.where(mine, pltpu.roll(low, turn, 1), to_low)
            to_high = jnp.where(mine, pltpu.roll(high, turn, 1), to_high)
    send[...] = flat[...].astype(jnp.bfloat16).reshape(send.shape)
    pack[0] = to_low[:, None, :]
    pack[1] = to_high[:, None, :]

    pl.semaphore_wait(
        barrier,
        devices - 1 + devices * (jnp.where(has_low, 1, 0) + jnp.where(has_high, 1, 0)),
    )

    def post(step):
        target = lax.rem(me + step + 1, devices)
        pltpu.make_async_remote_copy(
            src_ref=send.at[target], dst_ref=recv.at[me], send_sem=send_sem, recv_sem=recv_sem,
            device_id=(target, win), device_id_type=MESH,
        ).start()

    repeat(devices - 1, post)
    sides = (
        (has_low, -1, 0, from_high, high_sem),
        (has_high, 1, 1, from_low, low_sem),
    )
    for there, side, slot, landing, landed in sides:
        @pl.when(there)
        def _():
            def post_side(step):
                target = lax.rem(me + step, devices)
                pltpu.make_async_remote_copy(
                    src_ref=pack.at[slot, target], dst_ref=landing.at[me],
                    send_sem=pack_sem.at[slot], recv_sem=landed,
                    device_id=(target, win + side), device_id_type=MESH,
                ).start()

            repeat(devices, post_side)

    recv[me] = send[me]

    span = framed.shape[0]
    dips = spread_taps(dip_ref[...], devices, span)
    apart = (
        spread_places(shot_ref[...], devices, span)[0:1]
        - lax.broadcasted_iota(jnp.int32, (devices, span), 0) + reach
    )
    dip = jnp.zeros((devices, span), jnp.float32)
    for a in range(tap_count):
        dip = jnp.where(apart == a, dips[a : a + 1], dip)
    dip = dip.astype(jnp.bfloat16)

    for there, landing, landed in ((has_high, from_high, high_sem), (has_low, from_low, low_sem)):
        @pl.when(there)
        def _():
            pltpu.make_async_copy(landing, landing, landed).wait()

        @pl.when(jnp.logical_not(there))
        def _():
            landing[...] = jnp.zeros(landing.shape, jnp.float32)

    others = recv.at[pl.ds(0, devices - 1)]
    pltpu.make_async_copy(others, others, recv_sem).wait()

    rows[...] = recv[...].reshape(rows.shape).astype(jnp.float32)
    high_edge = from_high[...].reshape(devices, samples)
    low_edge = from_low[...].reshape(devices, samples)
    head, tail = lane < reach, lane >= samples - reach
    keep = (head & has_high) | (tail & has_low)
    for g in range(groups):
        turn = (samples - reach - g * stride) % samples
        high = pltpu.roll(high_edge, turn, 1)
        low = pltpu.roll(low_edge, turn, 1)
        inner = rows[pl.ds(g, devices, stride=2 * groups), :]
        outer = rows[pl.ds(groups + g, devices, stride=2 * groups), :]
        inner = inner + jnp.where(tail, high, jnp.where(head, low, 0.0))
        outer = jnp.where(keep, outer + jnp.where(head, high, low), 0.0)
        columns = slice(g * samples, (g + 1) * samples)
        for b in range(tap_count):
            move = b - reach
            if move > 0:
                both = jnp.where(lane < move, outer, inner)
            else:
                both = jnp.where(lane >= samples + move, outer, inner)
            turned = pltpu.roll(both, (-move) % samples, 1) if move else inner
            framed[b * devices : (b + 1) * devices, columns] = turned.astype(jnp.bfloat16)
    rest = span - tap_count * devices
    framed[tap_count * devices :, :] = jnp.zeros((rest, groups * samples), jnp.bfloat16)
    out_ref[...] = jnp.dot(dip, framed[...], preferred_element_type=jnp.float32).astype(jnp.bfloat16)

    sent = send.at[pl.ds(0, devices - 1)]
    pltpu.make_async_copy(sent, sent, send_sem).wait()
    for there, slot in ((has_low, 0), (has_high, 1)):
        @pl.when(there)
        def _():
            pltpu.make_async_copy(pack.at[slot], pack.at[slot], pack_sem.at[slot]).wait()


def on_device(devices, records, fan_taps, dip_taps, live_mask, node_place, shot_place):
    _, comps, nodes, samples = records.shape
    each = nodes // devices
    groups = comps * each
    slots = fan_taps.shape[1] + 1
    vmem = pl.BlockSpec(memory_space=pltpu.VMEM)
    result = pl.pallas_call(
        kernel,
        out_shape=jax.ShapeDtypeStruct((devices, groups * samples), jnp.bfloat16),
        in_specs=[pl.BlockSpec(memory_space=pl.ANY)] + [vmem] * 5,
        out_specs=vmem,
        scratch_shapes=[
            pltpu.VMEM((comps, nodes, samples), jnp.bfloat16),
            pltpu.VMEM((comps, nodes, slots * nodes), jnp.bfloat16),
            pltpu.VMEM((comps, slots * nodes, 2 * samples), jnp.bfloat16),
            pltpu.VMEM((slots * devices, groups * samples), jnp.bfloat16),
            pltpu.VMEM((devices, 2 * groups, samples), jnp.bfloat16),
            pltpu.VMEM((devices, 2 * groups, samples), jnp.bfloat16),
            pltpu.VMEM((devices * 2 * groups, samples), jnp.float32),
            pltpu.VMEM((devices * 2 * groups, samples), jnp.float32),
            pltpu.VMEM((2, devices, 1, samples), jnp.float32),
            pltpu.VMEM((devices, 1, samples), jnp.float32),
            pltpu.VMEM((devices, 1, samples), jnp.float32),
            pltpu.SemaphoreType.DMA,
            pltpu.SemaphoreType.DMA,
            pltpu.SemaphoreType.DMA,
            pltpu.SemaphoreType.DMA((2,)),
            pltpu.SemaphoreType.DMA,
            pltpu.SemaphoreType.DMA,
        ],
        compiler_params=pltpu.CompilerParams(
            collective_id=0, has_side_effects=True, vmem_limit_bytes=48 * 1024 * 1024
        ),
    )(records, fan_taps, dip_taps, live_mask, node_place[None], shot_place[None])
    return result.reshape(devices, comps, each, samples)


def solution(mesh):
    return jax.shard_map(
        functools.partial(on_device, mesh.shape["shot"]),
        mesh=mesh,
        in_specs=(P("shot", None, None, "tm"), P(), P(), P("shot", None), P(), P()),
        out_specs=P(None, None, "shot", "tm"),
        check_vma=False,
    )
```

```python
import functools

import jax
import jax.numpy as jnp
from jax import lax
from jax.experimental import pallas as pl
from jax.experimental.pallas import tpu as pltpu
from jax.sharding import PartitionSpec as P

MESH = pl.DeviceIdType.MESH


def repeat(count, body):
    if count <= 32:
        for step in range(count):
            body(step)
    else:
        lax.fori_loop(0, count, lambda step, carry: (body(step), carry)[1], 0)


def spread_taps(taps, groups, width):
    first = lax.broadcasted_iota(jnp.int32, (taps.shape[1], width), 0) * groups
    lane = lax.broadcasted_iota(jnp.int32, (taps.shape[1], width), 1)
    onehot = jnp.where((lane >= first) & (lane < first + groups), 1.0, 0.0).astype(jnp.bfloat16)
    return jnp.dot(taps, onehot, preferred_element_type=jnp.float32)


def spread_places(place, groups, width):
    row = lax.broadcasted_iota(jnp.int32, (groups, width), 0)
    lane = lax.broadcasted_iota(jnp.int32, (groups, width), 1)
    onehot = jnp.where(lax.rem(lane, groups) == row, 1.0, 0.0).astype(jnp.bfloat16)
    left = jnp.broadcast_to(place.astype(jnp.float32), (8, groups)).astype(jnp.bfloat16)
    return jnp.dot(left, onehot, preferred_element_type=jnp.float32).astype(jnp.int32)


def kernel(
    records_src, fan_src, dip_src, live_src, node_src, shot_src, out_ref,
    traces, fan_ref, dip_ref, live_ref, node_ref, shot_ref, matrix, shifted, framed, send, recv, flat, rows, pack, from_low, from_high,
    load_sem, send_sem, recv_sem, pack_sem, low_sem, high_sem,
):
    comps, nodes, samples = traces.shape
    devices = send.shape[0]
    each = nodes // devices
    groups = comps * each
    tap_count = dip_ref.shape[0]
    reach = (tap_count - 1) // 2
    me, win = lax.axis_index("shot"), lax.axis_index("tm")
    windows = lax.axis_size("tm")
    has_low, has_high = win > 0, win < windows - 1

    loads = [
        pltpu.make_async_copy(source, held, load_sem.at[i])
        for i, (source, held) in enumerate((
            (node_src, node_ref), (fan_src, fan_ref), (records_src.at[0], traces),
            (live_src, live_ref), (dip_src, dip_ref), (shot_src, shot_ref),
        ))
    ]
    for load in loads:
        load.start()

    barrier = pltpu.get_barrier_semaphore()

    def greet(step):
        pl.semaphore_signal(
            barrier, inc=1, device_id=(lax.rem(me + step + 1, devices), win), device_id_type=MESH
        )

    repeat(devices - 1, greet)
    for there, side in ((has_low, -1), (has_high, 1)):
        @pl.when(there)
        def _():
            repeat(devices, lambda step: pl.semaphore_signal(
                barrier, inc=1, device_id=(lax.rem(me + step, devices), win + side),
                device_id_type=MESH,
            ))

    depth = matrix.shape[2]
    loads[0].wait()
    loads[1].wait()
    tap_rows = fan_ref[...].astype(jnp.float32).reshape(tap_count * comps, tap_count)
    taps = spread_taps(tap_rows.astype(jnp.bfloat16), nodes, depth)
    places = spread_places(node_ref[...], nodes, depth)[0:1]
    block = min(devices, 16)

    def build(step):
        for j in range(each):
            at = (lax.broadcasted_iota(jnp.int32, (block, depth), 0) + step * block) * each + j
            apart = places - at + reach
            sums = [jnp.zeros((block, depth), jnp.float32)] * comps
            for a in range(tap_count):
                hit = apart == a
                sums = [jnp.where(hit, taps[a * comps + c : a * comps + c + 1], sums[c]) for c in range(comps)]
            for c in range(comps):
                start = j * devices + step * block
                if not isinstance(step, int):
                    start = pl.multiple_of(start, block)
                matrix[c, pl.ds(start, block), :] = sums[c].astype(jnp.bfloat16)

    if devices == block:
        build(0)
    else:
        lax.fori_loop(0, devices // block, lambda step, carry: (build(step), carry)[1], 0)

    loads[3].wait()
    position = lax.broadcasted_iota(jnp.int32, (devices, nodes), 0) * each
    alive = []
    for j in range(each):
        here = node_ref[...] == position + j
        kept = jnp.where(here, live_ref[...].astype(jnp.float32), 0.0)
        alive.append(jnp.sum(kept, axis=1, keepdims=True))

    loads[2].wait()
    lane = lax.broadcasted_iota(jnp.int32, (nodes, samples), 1)
    for c in range(comps):
        trace = traces[c].astype(jnp.float32)
        for b in range(tap_count):
            move = b - reach
            turned = pltpu.roll(trace, (-move) % samples, 1) if move else trace
            inside = (lane < samples - move) if move >= 0 else (lane >= -move)
            shifted[c, b * nodes : (b + 1) * nodes, :samples] = (
                jnp.where(inside, turned, 0.0).astype(jnp.bfloat16)
            )
            shifted[c, b * nodes : (b + 1) * nodes, samples:] = (
                jnp.where(inside, 0.0, turned).astype(jnp.bfloat16)
            )
        rest = depth - tap_count * nodes
        shifted[c, tap_count * nodes :, :] = jnp.zeros((rest, 2 * samples), jnp.bfloat16)

    lane = lax.broadcasted_iota(jnp.int32, (devices, samples), 1)
    stride = samples // groups
    to_low = jnp.zeros((devices, samples), jnp.float32)
    to_high = jnp.zeros((devices, samples), jnp.float32)
    for c in range(comps):
        field = jnp.dot(matrix[c], shifted[c], preferred_element_type=jnp.float32)
        for j in range(each):
            g = c * each + j
            part = field[j * devices : (j + 1) * devices] * alive[j]
            inner, outer = part[:, :samples], part[:, samples:]
            flat[pl.ds(g, devices, stride=2 * groups), :] = inner
            flat[pl.ds(groups + g, devices, stride=2 * groups), :] = outer
            mine = (lane >= g * stride) & (lane < g * stride + 2 * reach)
            turn = (reach + g * stride) % samples
            low = jnp.where(lane >= samples // 2, outer, inner)
            high = jnp.where(lane >= samples // 2, inner, outer)
            to_low = jnp.where(mine, pltpu.roll(low, turn, 1), to_low)
            to_high = jnp.where(mine, pltpu.roll(high, turn, 1), to_high)
    send[...] = flat[...].astype(jnp.bfloat16).reshape(send.shape)
    pack[0] = to_low[:, None, :]
    pack[1] = to_high[:, None, :]

    pl.semaphore_wait(
        barrier,
        devices - 1 + devices * (jnp.where(has_low, 1, 0) + jnp.where(has_high, 1, 0)),
    )

    def post(step):
        target = lax.rem(me + step + 1, devices)
        pltpu.make_async_remote_copy(
            src_ref=send.at[target], dst_ref=recv.at[me], send_sem=send_sem, recv_sem=recv_sem,
            device_id=(target, win), device_id_type=MESH,
        ).start()

    repeat(devices - 1, post)
    sides = (
        (has_low, -1, 0, from_high, high_sem),
        (has_high, 1, 1, from_low, low_sem),
    )
    for there, side, slot, landing, landed in sides:
        @pl.when(there)
        def _():
            def post_side(step):
                target = lax.rem(me + step, devices)
                pltpu.make_async_remote_copy(
                    src_ref=pack.at[slot, target], dst_ref=landing.at[me],
                    send_sem=pack_sem.at[slot], recv_sem=landed,
                    device_id=(target, win + side), device_id_type=MESH,
                ).start()

            repeat(devices, post_side)

    recv[me] = send[me]

    loads[4].wait()
    loads[5].wait()
    span = framed.shape[0]
    dips = spread_taps(dip_ref[...], devices, span)
    apart = (
        spread_places(shot_ref[...], devices, span)[0:1]
        - lax.broadcasted_iota(jnp.int32, (devices, span), 0) + reach
    )
    dip = jnp.zeros((devices, span), jnp.float32)
    for a in range(tap_count):
        dip = jnp.where(apart == a, dips[a : a + 1], dip)
    dip = dip.astype(jnp.bfloat16)

    for there, landing, landed in ((has_high, from_high, high_sem), (has_low, from_low, low_sem)):
        @pl.when(there)
        def _():
            pltpu.make_async_copy(landing, landing, landed).wait()

        @pl.when(jnp.logical_not(there))
        def _():
            landing[...] = jnp.zeros(landing.shape, jnp.float32)

    others = recv.at[pl.ds(0, devices - 1)]
    pltpu.make_async_copy(others, others, recv_sem).wait()

    rows[...] = recv[...].reshape(rows.shape).astype(jnp.float32)
    high_edge = from_high[...].reshape(devices, samples)
    low_edge = from_low[...].reshape(devices, samples)
    head, tail = lane < reach, lane >= samples - reach
    keep = (head & has_high) | (tail & has_low)
    for g in range(groups):
        turn = (samples - reach - g * stride) % samples
        high = pltpu.roll(high_edge, turn, 1)
        low = pltpu.roll(low_edge, turn, 1)
        inner = rows[pl.ds(g, devices, stride=2 * groups), :]
        outer = rows[pl.ds(groups + g, devices, stride=2 * groups), :]
        inner = inner + jnp.where(tail, high, jnp.where(head, low, 0.0))
        outer = jnp.where(keep, outer + jnp.where(head, high, low), 0.0)
        columns = slice(g * samples, (g + 1) * samples)
        for b in range(tap_count):
            move = b - reach
            if move > 0:
                both = jnp.where(lane < move, outer, inner)
            else:
                both = jnp.where(lane >= samples + move, outer, inner)
            turned = pltpu.roll(both, (-move) % samples, 1) if move else inner
            framed[b * devices : (b + 1) * devices, columns] = turned.astype(jnp.bfloat16)
    rest = span - tap_count * devices
    framed[tap_count * devices :, :] = jnp.zeros((rest, groups * samples), jnp.bfloat16)
    out_ref[...] = jnp.dot(dip, framed[...], preferred_element_type=jnp.float32).astype(jnp.bfloat16)

    sent = send.at[pl.ds(0, devices - 1)]
    pltpu.make_async_copy(sent, sent, send_sem).wait()
    for there, slot in ((has_low, 0), (has_high, 1)):
        @pl.when(there)
        def _():
            pltpu.make_async_copy(pack.at[slot], pack.at[slot], pack_sem.at[slot]).wait()


def on_device(devices, records, fan_taps, dip_taps, live_mask, node_place, shot_place):
    _, comps, nodes, samples = records.shape
    each = nodes // devices
    groups = comps * each
    slots = fan_taps.shape[1] + 1
    vmem = pl.BlockSpec(memory_space=pltpu.VMEM)
    result = pl.pallas_call(
        kernel,
        out_shape=jax.ShapeDtypeStruct((devices, groups * samples), jnp.bfloat16),
        in_specs=[pl.BlockSpec(memory_space=pl.ANY)] * 6,
        out_specs=vmem,
        scratch_shapes=[
            pltpu.VMEM((comps, nodes, samples), jnp.bfloat16),
            pltpu.VMEM((slots - 1, comps, slots - 1), jnp.bfloat16),
            pltpu.VMEM(dip_taps.shape, jnp.bfloat16),
            pltpu.VMEM((1, nodes), jnp.int32),
            pltpu.VMEM((1, nodes), jnp.int32),
            pltpu.VMEM((1, devices), jnp.int32),
            pltpu.VMEM((comps, nodes, slots * nodes), jnp.bfloat16),
            pltpu.VMEM((comps, slots * nodes, 2 * samples), jnp.bfloat16),
            pltpu.VMEM((slots * devices, groups * samples), jnp.bfloat16),
            pltpu.VMEM((devices, 2 * groups, samples), jnp.bfloat16),
            pltpu.VMEM((devices, 2 * groups, samples), jnp.bfloat16),
            pltpu.VMEM((devices * 2 * groups, samples), jnp.float32),
            pltpu.VMEM((devices * 2 * groups, samples), jnp.float32),
            pltpu.VMEM((2, devices, 1, samples), jnp.float32),
            pltpu.VMEM((devices, 1, samples), jnp.float32),
            pltpu.VMEM((devices, 1, samples), jnp.float32),
            pltpu.SemaphoreType.DMA((6,)),
            pltpu.SemaphoreType.DMA,
            pltpu.SemaphoreType.DMA,
            pltpu.SemaphoreType.DMA((2,)),
            pltpu.SemaphoreType.DMA,
            pltpu.SemaphoreType.DMA,
        ],
        compiler_params=pltpu.CompilerParams(
            collective_id=0, has_side_effects=True, vmem_limit_bytes=60 * 1024 * 1024
        ),
    )(records, fan_taps.transpose(1, 0, 2), dip_taps, live_mask, node_place[None], shot_place[None])
    return result.reshape(devices, comps, each, samples)


def solution(mesh):
    return jax.shard_map(
        functools.partial(on_device, mesh.shape["shot"]),
        mesh=mesh,
        in_specs=(P("shot", None, None, "tm"), P(), P(), P("shot", None), P(), P()),
        out_specs=P(None, None, "shot", "tm"),
        check_vma=False,
    )
```

```python
import functools

import jax
import jax.numpy as jnp
from jax import lax
from jax.experimental import pallas as pl
from jax.experimental.pallas import tpu as pltpu
from jax.sharding import PartitionSpec as P

MESH = pl.DeviceIdType.MESH


def repeat(count, body):
    if count <= 32:
        for step in range(count):
            body(step)
    else:
        lax.fori_loop(0, count, lambda step, carry: (body(step), carry)[1], 0)


def spread_taps(taps, groups, width):
    first = lax.broadcasted_iota(jnp.int32, (taps.shape[1], width), 0) * groups
    lane = lax.broadcasted_iota(jnp.int32, (taps.shape[1], width), 1)
    onehot = jnp.where((lane >= first) & (lane < first + groups), 1.0, 0.0).astype(jnp.bfloat16)
    return jnp.dot(taps, onehot, preferred_element_type=jnp.float32)


def spread_places(place, groups, width):
    row = lax.broadcasted_iota(jnp.int32, (groups, width), 0)
    lane = lax.broadcasted_iota(jnp.int32, (groups, width), 1)
    onehot = jnp.where(lax.rem(lane, groups) == row, 1.0, 0.0).astype(jnp.bfloat16)
    left = jnp.broadcast_to(place.astype(jnp.float32), (8, groups)).astype(jnp.bfloat16)
    return jnp.dot(left, onehot, preferred_element_type=jnp.float32).astype(jnp.int32)


def kernel(
    traces, taps_ref, live_ref, node_ref, shot_ref, out_ref,
    matrix, shifted, framed, send, recv, flat, rows, pack, from_low, from_high,
    send_sem, recv_sem, pack_sem, low_sem, high_sem,
):
    _, comps, nodes, samples = traces.shape
    devices = send.shape[0]
    each = nodes // devices
    groups = comps * each
    tap_count = taps_ref.shape[1]
    reach = (tap_count - 1) // 2
    me, win = lax.axis_index("shot"), lax.axis_index("tm")
    windows = lax.axis_size("tm")
    has_low, has_high = win > 0, win < windows - 1

    barrier = pltpu.get_barrier_semaphore()

    def greet(step):
        pl.semaphore_signal(
            barrier, inc=1, device_id=(lax.rem(me + step + 1, devices), win), device_id_type=MESH
        )

    repeat(devices - 1, greet)
    for there, side in ((has_low, -1), (has_high, 1)):
        @pl.when(there)
        def _():
            repeat(devices, lambda step: pl.semaphore_signal(
                barrier, inc=1, device_id=(lax.rem(me + step, devices), win + side),
                device_id_type=MESH,
            ))

    depth = matrix.shape[2]
    taps = [spread_taps(taps_ref[c], nodes, depth) for c in range(comps)]
    places = spread_places(node_ref[...], nodes, depth)[0:1]
    block = min(devices, 16)

    def build(step):
        for j in range(each):
            at = (lax.broadcasted_iota(jnp.int32, (block, depth), 0) + step * block) * each + j
            apart = places - at + reach
            sums = [jnp.zeros((block, depth), jnp.float32)] * comps
            for a in range(tap_count):
                hit = apart == a
                sums = [jnp.where(hit, taps[c][a : a + 1], sums[c]) for c in range(comps)]
            for c in range(comps):
                start = j * devices + step * block
                if not isinstance(step, int):
                    start = pl.multiple_of(start, block)
                matrix[c, pl.ds(start, block), :] = sums[c].astype(jnp.bfloat16)

    if devices == block:
        build(0)
    else:
        lax.fori_loop(0, devices // block, lambda step, carry: (build(step), carry)[1], 0)

    position = lax.broadcasted_iota(jnp.int32, (devices, nodes), 0) * each
    alive = []
    for j in range(each):
        here = node_ref[...] == position + j
        kept = jnp.where(here, live_ref[...].astype(jnp.float32), 0.0)
        alive.append(jnp.sum(kept, axis=1, keepdims=True))

    lane = lax.broadcasted_iota(jnp.int32, (nodes, samples), 1)
    for c in range(comps):
        trace = traces[0, c]
        for b in range(tap_count):
            move = b - reach
            turned = pltpu.roll(trace, (-move) % samples, 1) if move else trace
            inside = (lane < samples - move) if move >= 0 else (lane >= -move)
            shifted[c, b * nodes : (b + 1) * nodes, :samples] = (
                jnp.where(inside, turned, jnp.bfloat16(0))
            )
            shifted[c, b * nodes : (b + 1) * nodes, samples:] = (
                jnp.where(inside, jnp.bfloat16(0), turned)
            )
        rest = depth - tap_count * nodes
        shifted[c, tap_count * nodes :, :] = jnp.zeros((rest, 2 * samples), jnp.bfloat16)

    lane = lax.broadcasted_iota(jnp.int32, (devices, samples), 1)
    stride = samples // groups
    to_low = jnp.zeros((devices, samples), jnp.float32)
    to_high = jnp.zeros((devices, samples), jnp.float32)
    for c in range(comps):
        field = jnp.dot(matrix[c], shifted[c], preferred_element_type=jnp.float32)
        for j in range(each):
            g = c * each + j
            part = field[j * devices : (j + 1) * devices] * alive[j]
            inner, outer = part[:, :samples], part[:, samples:]
            flat[pl.ds(g, devices, stride=2 * groups), :] = inner
            flat[pl.ds(groups + g, devices, stride=2 * groups), :] = outer
            mine = (lane >= g * stride) & (lane < g * stride + 2 * reach)
            turn = (reach + g * stride) % samples
            low = jnp.where(lane >= samples // 2, outer, inner)
            high = jnp.where(lane >= samples // 2, inner, outer)
            to_low = jnp.where(mine, pltpu.roll(low, turn, 1), to_low)
            to_high = jnp.where(mine, pltpu.roll(high, turn, 1), to_high)
    send[...] = flat[...].astype(jnp.bfloat16).reshape(send.shape)
    pack[0] = to_low[:, None, :]
    pack[1] = to_high[:, None, :]

    pl.semaphore_wait(
        barrier,
        devices - 1 + devices * (jnp.where(has_low, 1, 0) + jnp.where(has_high, 1, 0)),
    )

    def post(step):
        target = lax.rem(me + step + 1, devices)
        pltpu.make_async_remote_copy(
            src_ref=send.at[target], dst_ref=recv.at[me], send_sem=send_sem, recv_sem=recv_sem,
            device_id=(target, win), device_id_type=MESH,
        ).start()

    repeat(devices - 1, post)
    sides = (
        (has_low, -1, 0, from_high, high_sem),
        (has_high, 1, 1, from_low, low_sem),
    )
    for there, side, slot, landing, landed in sides:
        @pl.when(there)
        def _():
            def post_side(step):
                target = lax.rem(me + step, devices)
                pltpu.make_async_remote_copy(
                    src_ref=pack.at[slot, target], dst_ref=landing.at[me],
                    send_sem=pack_sem.at[slot], recv_sem=landed,
                    device_id=(target, win + side), device_id_type=MESH,
                ).start()

            repeat(devices, post_side)

    recv[me] = send[me]

    span = framed.shape[0]
    dips = spread_taps(taps_ref[comps], devices, span)
    apart = (
        spread_places(shot_ref[...], devices, span)[0:1]
        - lax.broadcasted_iota(jnp.int32, (devices, span), 0) + reach
    )
    dip = jnp.zeros((devices, span), jnp.float32)
    for a in range(tap_count):
        dip = jnp.where(apart == a, dips[a : a + 1], dip)
    dip = dip.astype(jnp.bfloat16)

    for there, landing, landed in ((has_high, from_high, high_sem), (has_low, from_low, low_sem)):
        @pl.when(there)
        def _():
            pltpu.make_async_copy(landing, landing, landed).wait()

        @pl.when(jnp.logical_not(there))
        def _():
            landing[...] = jnp.zeros(landing.shape, jnp.float32)

    others = recv.at[pl.ds(0, devices - 1)]
    pltpu.make_async_copy(others, others, recv_sem).wait()

    rows[...] = recv[...].reshape(rows.shape).astype(jnp.float32)
    high_edge = from_high[...].reshape(devices, samples)
    low_edge = from_low[...].reshape(devices, samples)
    head, tail = lane < reach, lane >= samples - reach
    keep = (head & has_high) | (tail & has_low)
    for g in range(groups):
        turn = (samples - reach - g * stride) % samples
        high = pltpu.roll(high_edge, turn, 1)
        low = pltpu.roll(low_edge, turn, 1)
        inner = rows[pl.ds(g, devices, stride=2 * groups), :]
        outer = rows[pl.ds(groups + g, devices, stride=2 * groups), :]
        inner = inner + jnp.where(tail, high, jnp.where(head, low, 0.0))
        outer = jnp.where(keep, outer + jnp.where(head, high, low), 0.0)
        inner, outer = inner.astype(jnp.bfloat16), outer.astype(jnp.bfloat16)
        columns = slice(g * samples, (g + 1) * samples)
        for b in range(tap_count):
            move = b - reach
            if move > 0:
                both = jnp.where(lane < move, outer, inner)
            else:
                both = jnp.where(lane >= samples + move, outer, inner)
            turned = pltpu.roll(both, (-move) % samples, 1) if move else inner
            framed[b * devices : (b + 1) * devices, columns] = turned
    rest = span - tap_count * devices
    framed[tap_count * devices :, :] = jnp.zeros((rest, groups * samples), jnp.bfloat16)
    out_ref[...] = jnp.dot(dip, framed[...], preferred_element_type=jnp.float32).astype(jnp.bfloat16)

    sent = send.at[pl.ds(0, devices - 1)]
    pltpu.make_async_copy(sent, sent, send_sem).wait()
    for there, slot in ((has_low, 0), (has_high, 1)):
        @pl.when(there)
        def _():
            pltpu.make_async_copy(pack.at[slot], pack.at[slot], pack_sem.at[slot]).wait()


def on_device(devices, records, fan_taps, dip_taps, live_mask, node_place, shot_place):
    _, comps, nodes, samples = records.shape
    each = nodes // devices
    groups = comps * each
    slots = fan_taps.shape[1] + 1
    taps = jnp.concatenate([fan_taps, dip_taps[None]])
    vmem = pl.BlockSpec(memory_space=pltpu.VMEM)
    result = pl.pallas_call(
        kernel,
        out_shape=jax.ShapeDtypeStruct((devices, groups * samples), jnp.bfloat16),
        in_specs=[vmem] * 5,
        out_specs=vmem,
        scratch_shapes=[
            pltpu.VMEM((comps, nodes, slots * nodes), jnp.bfloat16),
            pltpu.VMEM((comps, slots * nodes, 2 * samples), jnp.bfloat16),
            pltpu.VMEM((slots * devices, groups * samples), jnp.bfloat16),
            pltpu.VMEM((devices, 2 * groups, samples), jnp.bfloat16),
            pltpu.VMEM((devices, 2 * groups, samples), jnp.bfloat16),
            pltpu.VMEM((devices * 2 * groups, samples), jnp.float32),
            pltpu.VMEM((devices * 2 * groups, samples), jnp.float32),
            pltpu.VMEM((2, devices, 1, samples), jnp.float32),
            pltpu.VMEM((devices, 1, samples), jnp.float32),
            pltpu.VMEM((devices, 1, samples), jnp.float32),
            pltpu.SemaphoreType.DMA,
            pltpu.SemaphoreType.DMA,
            pltpu.SemaphoreType.DMA((2,)),
            pltpu.SemaphoreType.DMA,
            pltpu.SemaphoreType.DMA,
        ],
        compiler_params=pltpu.CompilerParams(
            collective_id=0, has_side_effects=True, vmem_limit_bytes=48 * 1024 * 1024
        ),
    )(records, taps, live_mask, node_place[None], shot_place[None])
    return result.reshape(devices, comps, each, samples)


def solution(mesh):
    return jax.shard_map(
        functools.partial(on_device, mesh.shape["shot"]),
        mesh=mesh,
        in_specs=(P("shot", None, None, "tm"), P(), P(), P("shot", None), P(), P()),
        out_specs=P(None, None, "shot", "tm"),
        check_vma=False,
    )
```

```python
import functools

import jax
import jax.numpy as jnp
from jax import lax
from jax.experimental import pallas as pl
from jax.experimental.pallas import tpu as pltpu
from jax.sharding import PartitionSpec as P

MESH = pl.DeviceIdType.MESH


def repeat(count, body):
    if count <= 32:
        for step in range(count):
            body(step)
    else:
        lax.fori_loop(0, count, lambda step, carry: (body(step), carry)[1], 0)


def far_first(step, count):
    return count // 2 + (1 - 2 * (step % 2)) * ((step + 1) // 2)


def spread_taps(taps, groups, width):
    first = lax.broadcasted_iota(jnp.int32, (taps.shape[1], width), 0) * groups
    lane = lax.broadcasted_iota(jnp.int32, (taps.shape[1], width), 1)
    onehot = jnp.where((lane >= first) & (lane < first + groups), 1.0, 0.0).astype(jnp.bfloat16)
    return jnp.dot(taps, onehot, preferred_element_type=jnp.float32)


def spread_places(place, groups, width):
    row = lax.broadcasted_iota(jnp.int32, (groups, width), 0)
    lane = lax.broadcasted_iota(jnp.int32, (groups, width), 1)
    onehot = jnp.where(lax.rem(lane, groups) == row, 1.0, 0.0).astype(jnp.bfloat16)
    left = jnp.broadcast_to(place.astype(jnp.float32), (8, groups)).astype(jnp.bfloat16)
    return jnp.dot(left, onehot, preferred_element_type=jnp.float32).astype(jnp.int32)


def kernel(
    traces, taps_ref, live_ref, node_ref, shot_ref, out_ref,
    matrix, shifted, framed, send, recv, flat, rows, pack, from_low, from_high,
    send_sem, recv_sem, pack_sem, low_sem, high_sem,
):
    _, comps, nodes, samples = traces.shape
    devices = send.shape[0]
    each = nodes // devices
    groups = comps * each
    tap_count = taps_ref.shape[1]
    reach = (tap_count - 1) // 2
    me, win = lax.axis_index("shot"), lax.axis_index("tm")
    windows = lax.axis_size("tm")
    has_low, has_high = win > 0, win < windows - 1

    barrier = pltpu.get_barrier_semaphore()

    def greet(step):
        pl.semaphore_signal(
            barrier, inc=1, device_id=(lax.rem(me + far_first(step, devices), devices), win), device_id_type=MESH
        )

    repeat(devices - 1, greet)
    for there, side in ((has_low, -1), (has_high, 1)):
        @pl.when(there)
        def _():
            repeat(devices, lambda step: pl.semaphore_signal(
                barrier, inc=1, device_id=(lax.rem(me + far_first(step, devices), devices), win + side),
                device_id_type=MESH,
            ))

    depth = matrix.shape[2]
    taps = [spread_taps(taps_ref[c], nodes, depth) for c in range(comps)]
    places = spread_places(node_ref[...], nodes, depth)[0:1]
    block = min(devices, 16)

    def build(step):
        for j in range(each):
            at = (lax.broadcasted_iota(jnp.int32, (block, depth), 0) + step * block) * each + j
            apart = places - at + reach
            sums = [jnp.zeros((block, depth), jnp.float32)] * comps
            for a in range(tap_count):
                hit = apart == a
                sums = [jnp.where(hit, taps[c][a : a + 1], sums[c]) for c in range(comps)]
            for c in range(comps):
                start = j * devices + step * block
                if not isinstance(step, int):
                    start = pl.multiple_of(start, block)
                matrix[c, pl.ds(start, block), :] = sums[c].astype(jnp.bfloat16)

    if devices == block:
        build(0)
    else:
        lax.fori_loop(0, devices // block, lambda step, carry: (build(step), carry)[1], 0)

    position = lax.broadcasted_iota(jnp.int32, (devices, nodes), 0) * each
    alive = []
    for j in range(each):
        here = node_ref[...] == position + j
        kept = jnp.where(here, live_ref[...].astype(jnp.float32), 0.0)
        alive.append(jnp.sum(kept, axis=1, keepdims=True))

    lane = lax.broadcasted_iota(jnp.int32, (nodes, samples), 1)
    for c in range(comps):
        trace = traces[0, c]
        for b in range(tap_count):
            move = b - reach
            turned = pltpu.roll(trace, (-move) % samples, 1) if move else trace
            inside = (lane < samples - move) if move >= 0 else (lane >= -move)
            shifted[c, b * nodes : (b + 1) * nodes, :samples] = (
                jnp.where(inside, turned, jnp.bfloat16(0))
            )
            shifted[c, b * nodes : (b + 1) * nodes, samples:] = (
                jnp.where(inside, jnp.bfloat16(0), turned)
            )
        rest = depth - tap_count * nodes
        shifted[c, tap_count * nodes :, :] = jnp.zeros((rest, 2 * samples), jnp.bfloat16)

    lane = lax.broadcasted_iota(jnp.int32, (devices, samples), 1)
    stride = samples // groups
    to_low = jnp.zeros((devices, samples), jnp.float32)
    to_high = jnp.zeros((devices, samples), jnp.float32)
    for c in range(comps):
        field = jnp.dot(matrix[c], shifted[c], preferred_element_type=jnp.float32)
        for j in range(each):
            g = c * each + j
            part = field[j * devices : (j + 1) * devices] * alive[j]
            inner, outer = part[:, :samples], part[:, samples:]
            flat[pl.ds(g, devices, stride=2 * groups), :] = inner
            flat[pl.ds(groups + g, devices, stride=2 * groups), :] = outer
            mine = (lane >= g * stride) & (lane < g * stride + 2 * reach)
            turn = (reach + g * stride) % samples
            low = jnp.where(lane >= samples // 2, outer, inner)
            high = jnp.where(lane >= samples // 2, inner, outer)
            to_low = jnp.where(mine, pltpu.roll(low, turn, 1), to_low)
            to_high = jnp.where(mine, pltpu.roll(high, turn, 1), to_high)
    send[...] = flat[...].astype(jnp.bfloat16).reshape(send.shape)
    pack[0] = to_low[:, None, :]
    pack[1] = to_high[:, None, :]

    pl.semaphore_wait(
        barrier,
        devices - 1 + devices * (jnp.where(has_low, 1, 0) + jnp.where(has_high, 1, 0)),
    )

    def post(step):
        target = lax.rem(me + far_first(step, devices), devices)
        pltpu.make_async_remote_copy(
            src_ref=send.at[target], dst_ref=recv.at[me], send_sem=send_sem, recv_sem=recv_sem,
            device_id=(target, win), device_id_type=MESH,
        ).start()

    sides = (
        (has_low, -1, 0, from_high, high_sem),
        (has_high, 1, 1, from_low, low_sem),
    )
    for there, side, slot, landing, landed in sides:
        @pl.when(there)
        def _():
            def post_side(step):
                target = lax.rem(me + far_first(step, devices), devices)
                pltpu.make_async_remote_copy(
                    src_ref=pack.at[slot, target], dst_ref=landing.at[me],
                    send_sem=pack_sem.at[slot], recv_sem=landed,
                    device_id=(target, win + side), device_id_type=MESH,
                ).start()

            repeat(devices, post_side)

    repeat(devices - 1, post)
    recv[me] = send[me]

    span = framed.shape[0]
    dips = spread_taps(taps_ref[comps], devices, span)
    apart = (
        spread_places(shot_ref[...], devices, span)[0:1]
        - lax.broadcasted_iota(jnp.int32, (devices, span), 0) + reach
    )
    dip = jnp.zeros((devices, span), jnp.float32)
    for a in range(tap_count):
        dip = jnp.where(apart == a, dips[a : a + 1], dip)
    dip = dip.astype(jnp.bfloat16)

    for there, landing, landed in ((has_high, from_high, high_sem), (has_low, from_low, low_sem)):
        @pl.when(there)
        def _():
            pltpu.make_async_copy(landing, landing, landed).wait()

        @pl.when(jnp.logical_not(there))
        def _():
            landing[...] = jnp.zeros(landing.shape, jnp.float32)

    others = recv.at[pl.ds(0, devices - 1)]
    pltpu.make_async_copy(others, others, recv_sem).wait()

    rows[...] = recv[...].reshape(rows.shape).astype(jnp.float32)
    high_edge = from_high[...].reshape(devices, samples)
    low_edge = from_low[...].reshape(devices, samples)
    head, tail = lane < reach, lane >= samples - reach
    keep = (head & has_high) | (tail & has_low)
    for g in range(groups):
        turn = (samples - reach - g * stride) % samples
        high = pltpu.roll(high_edge, turn, 1)
        low = pltpu.roll(low_edge, turn, 1)
        inner = rows[pl.ds(g, devices, stride=2 * groups), :]
        outer = rows[pl.ds(groups + g, devices, stride=2 * groups), :]
        inner = inner + jnp.where(tail, high, jnp.where(head, low, 0.0))
        outer = jnp.where(keep, outer + jnp.where(head, high, low), 0.0)
        inner, outer = inner.astype(jnp.bfloat16), outer.astype(jnp.bfloat16)
        columns = slice(g * samples, (g + 1) * samples)
        for b in range(tap_count):
            move = b - reach
            if move > 0:
                both = jnp.where(lane < move, outer, inner)
            else:
                both = jnp.where(lane >= samples + move, outer, inner)
            turned = pltpu.roll(both, (-move) % samples, 1) if move else inner
            framed[b * devices : (b + 1) * devices, columns] = turned
    rest = span - tap_count * devices
    framed[tap_count * devices :, :] = jnp.zeros((rest, groups * samples), jnp.bfloat16)
    out_ref[...] = jnp.dot(dip, framed[...], preferred_element_type=jnp.float32).astype(jnp.bfloat16)

    sent = send.at[pl.ds(0, devices - 1)]
    pltpu.make_async_copy(sent, sent, send_sem).wait()
    for there, slot in ((has_low, 0), (has_high, 1)):
        @pl.when(there)
        def _():
            pltpu.make_async_copy(pack.at[slot], pack.at[slot], pack_sem.at[slot]).wait()


def on_device(devices, records, fan_taps, dip_taps, live_mask, node_place, shot_place):
    _, comps, nodes, samples = records.shape
    each = nodes // devices
    groups = comps * each
    slots = fan_taps.shape[1] + 1
    taps = jnp.concatenate([fan_taps, dip_taps[None]])
    vmem = pl.BlockSpec(memory_space=pltpu.VMEM)
    result = pl.pallas_call(
        kernel,
        out_shape=jax.ShapeDtypeStruct((devices, groups * samples), jnp.bfloat16),
        in_specs=[vmem] * 5,
        out_specs=vmem,
        scratch_shapes=[
            pltpu.VMEM((comps, nodes, slots * nodes), jnp.bfloat16),
            pltpu.VMEM((comps, slots * nodes, 2 * samples), jnp.bfloat16),
            pltpu.VMEM((slots * devices, groups * samples), jnp.bfloat16),
            pltpu.VMEM((devices, 2 * groups, samples), jnp.bfloat16),
            pltpu.VMEM((devices, 2 * groups, samples), jnp.bfloat16),
            pltpu.VMEM((devices * 2 * groups, samples), jnp.float32),
            pltpu.VMEM((devices * 2 * groups, samples), jnp.float32),
            pltpu.VMEM((2, devices, 1, samples), jnp.float32),
            pltpu.VMEM((devices, 1, samples), jnp.float32),
            pltpu.VMEM((devices, 1, samples), jnp.float32),
            pltpu.SemaphoreType.DMA,
            pltpu.SemaphoreType.DMA,
            pltpu.SemaphoreType.DMA((2,)),
            pltpu.SemaphoreType.DMA,
            pltpu.SemaphoreType.DMA,
        ],
        compiler_params=pltpu.CompilerParams(
            collective_id=0, has_side_effects=True, vmem_limit_bytes=48 * 1024 * 1024
        ),
    )(records, taps, live_mask, node_place[None], shot_place[None])
    return result.reshape(devices, comps, each, samples)


def solution(mesh):
    return jax.shard_map(
        functools.partial(on_device, mesh.shape["shot"]),
        mesh=mesh,
        in_specs=(P("shot", None, None, "tm"), P(), P(), P("shot", None), P(), P()),
        out_specs=P(None, None, "shot", "tm"),
        check_vma=False,
    )
```

```python
import functools

import jax
import jax.numpy as jnp
from jax import lax
from jax.experimental import pallas as pl
from jax.experimental.pallas import tpu as pltpu
from jax.sharding import PartitionSpec as P

MESH = pl.DeviceIdType.MESH


def repeat(count, body):
    if count <= 32:
        for step in range(count):
            body(step)
    else:
        lax.fori_loop(0, count, lambda step, carry: (body(step), carry)[1], 0)


def far_first(step, count):
    return count // 2 + (1 - 2 * (step % 2)) * ((step + 1) // 2)


def spread_taps(taps, groups, width):
    first = lax.broadcasted_iota(jnp.int32, (taps.shape[1], width), 0) * groups
    lane = lax.broadcasted_iota(jnp.int32, (taps.shape[1], width), 1)
    onehot = jnp.where((lane >= first) & (lane < first + groups), 1.0, 0.0).astype(jnp.bfloat16)
    return jnp.dot(taps, onehot, preferred_element_type=jnp.float32)


def spread_places(place, groups, width):
    row = lax.broadcasted_iota(jnp.int32, (groups, width), 0)
    lane = lax.broadcasted_iota(jnp.int32, (groups, width), 1)
    onehot = jnp.where(lax.rem(lane, groups) == row, 1.0, 0.0).astype(jnp.bfloat16)
    left = jnp.broadcast_to(place.astype(jnp.float32), (8, groups)).astype(jnp.bfloat16)
    return jnp.dot(left, onehot, preferred_element_type=jnp.float32).astype(jnp.int32)


def kernel(
    traces, taps_ref, live_ref, node_ref, shot_ref, out_ref,
    matrix, shifted, framed, send, recv, flat, rows, pack, from_low, from_high,
    send_sem, recv_sem, pack_sem, low_sem, high_sem,
):
    _, comps, nodes, samples = traces.shape
    devices = send.shape[0]
    each = nodes // devices
    groups = comps * each
    tap_count = taps_ref.shape[1]
    reach = (tap_count - 1) // 2
    me, win = lax.axis_index("shot"), lax.axis_index("tm")
    windows = lax.axis_size("tm")
    has_low, has_high = win > 0, win < windows - 1

    barrier = pltpu.get_barrier_semaphore()

    def greet(step):
        pl.semaphore_signal(
            barrier, inc=1, device_id=(lax.rem(me + far_first(step, devices), devices), win), device_id_type=MESH
        )

    repeat(devices - 1, greet)
    for there, side in ((has_low, -1), (has_high, 1)):
        @pl.when(there)
        def _():
            repeat(devices, lambda step: pl.semaphore_signal(
                barrier, inc=1, device_id=(lax.rem(me + far_first(step, devices), devices), win + side),
                device_id_type=MESH,
            ))

    depth = matrix.shape[2]
    taps = [spread_taps(taps_ref[c], nodes, depth) for c in range(comps)]
    places = spread_places(node_ref[...], nodes, depth)[0:1]
    block = min(devices, 16)

    def build(step):
        for j in range(each):
            at = (lax.broadcasted_iota(jnp.int32, (block, depth), 0) + step * block) * each + j
            apart = places - at + reach
            sums = [jnp.zeros((block, depth), jnp.float32)] * comps
            for a in range(tap_count):
                hit = apart == a
                sums = [jnp.where(hit, taps[c][a : a + 1], sums[c]) for c in range(comps)]
            for c in range(comps):
                start = j * devices + step * block
                if not isinstance(step, int):
                    start = pl.multiple_of(start, block)
                matrix[c, pl.ds(start, block), :] = sums[c].astype(jnp.bfloat16)

    if devices == block:
        build(0)
    else:
        lax.fori_loop(0, devices // block, lambda step, carry: (build(step), carry)[1], 0)

    position = lax.broadcasted_iota(jnp.int32, (devices, nodes), 0) * each
    alive = []
    for j in range(each):
        here = node_ref[...] == position + j
        kept = jnp.where(here, live_ref[...].astype(jnp.float32), 0.0)
        alive.append(jnp.sum(kept, axis=1, keepdims=True))

    lane = lax.broadcasted_iota(jnp.int32, (nodes, samples), 1)
    for c in range(comps):
        trace = traces[0, c]
        for b in range(tap_count):
            move = b - reach
            turned = pltpu.roll(trace, (-move) % samples, 1) if move else trace
            inside = (lane < samples - move) if move >= 0 else (lane >= -move)
            shifted[c, b * nodes : (b + 1) * nodes, :samples] = (
                jnp.where(inside, turned, jnp.bfloat16(0))
            )
            shifted[c, b * nodes : (b + 1) * nodes, samples:] = (
                jnp.where(inside, jnp.bfloat16(0), turned)
            )
        rest = depth - tap_count * nodes
        shifted[c, tap_count * nodes :, :] = jnp.zeros((rest, 2 * samples), jnp.bfloat16)

    lane = lax.broadcasted_iota(jnp.int32, (devices, samples), 1)
    stride = samples // groups
    to_low = jnp.zeros((devices, samples), jnp.float32)
    to_high = jnp.zeros((devices, samples), jnp.float32)
    for c in range(comps):
        field = jnp.dot(matrix[c], shifted[c], preferred_element_type=jnp.float32)
        for j in range(each):
            g = c * each + j
            part = field[j * devices : (j + 1) * devices] * alive[j]
            inner, outer = part[:, :samples], part[:, samples:]
            flat[pl.ds(g, devices, stride=2 * groups), :] = inner
            flat[pl.ds(groups + g, devices, stride=2 * groups), :] = outer
            mine = (lane >= g * stride) & (lane < g * stride + 2 * reach)
            turn = (reach + g * stride) % samples
            low = jnp.where(lane >= samples // 2, outer, inner)
            high = jnp.where(lane >= samples // 2, inner, outer)
            to_low = jnp.where(mine, pltpu.roll(low, turn, 1), to_low)
            to_high = jnp.where(mine, pltpu.roll(high, turn, 1), to_high)
    send[...] = flat[...].astype(jnp.bfloat16).reshape(send.shape)
    pack[0] = to_low[:, None, :]
    pack[1] = to_high[:, None, :]

    pl.semaphore_wait(
        barrier,
        devices - 1 + devices * (jnp.where(has_low, 1, 0) + jnp.where(has_high, 1, 0)),
    )

    def post(step):
        target = lax.rem(me + far_first(step, devices), devices)
        pltpu.make_async_remote_copy(
            src_ref=send.at[target], dst_ref=recv.at[me], send_sem=send_sem, recv_sem=recv_sem,
            device_id=(target, win), device_id_type=MESH,
        ).start()

    sides = (
        (has_low, -1, 0, from_high, high_sem),
        (has_high, 1, 1, from_low, low_sem),
    )
    for there, side, slot, landing, landed in sides:
        @pl.when(there)
        def _():
            def post_side(step):
                target = lax.rem(me + far_first(step, devices), devices)
                pltpu.make_async_remote_copy(
                    src_ref=pack.at[slot, target], dst_ref=landing.at[me],
                    send_sem=pack_sem.at[slot], recv_sem=landed,
                    device_id=(target, win + side), device_id_type=MESH,
                ).start()

            repeat(devices, post_side)

    repeat(devices - 1, post)
    recv[me] = send[me]

    span = framed.shape[0]
    dips = spread_taps(taps_ref[comps], devices, span)
    apart = (
        spread_places(shot_ref[...], devices, span)[0:1]
        - lax.broadcasted_iota(jnp.int32, (devices, span), 0) + reach
    )
    dip = jnp.zeros((devices, span), jnp.float32)
    for a in range(tap_count):
        dip = jnp.where(apart == a, dips[a : a + 1], dip)
    dip = dip.astype(jnp.bfloat16)

    rest = span - tap_count * devices
    framed[tap_count * devices :, :] = jnp.zeros((rest, groups * samples), jnp.bfloat16)

    for there, landing, landed in ((has_high, from_high, high_sem), (has_low, from_low, low_sem)):
        @pl.when(there)
        def _():
            pltpu.make_async_copy(landing, landing, landed).wait()

        @pl.when(jnp.logical_not(there))
        def _():
            landing[...] = jnp.zeros(landing.shape, jnp.float32)

    others = recv.at[pl.ds(0, devices - 1)]
    pltpu.make_async_copy(others, others, recv_sem).wait()

    rows[...] = recv[...].reshape(rows.shape).astype(jnp.float32)
    high_edge = from_high[...].reshape(devices, samples)
    low_edge = from_low[...].reshape(devices, samples)
    head, tail = lane < reach, lane >= samples - reach
    keep = (head & has_high) | (tail & has_low)
    for g in range(groups):
        turn = (samples - reach - g * stride) % samples
        high = pltpu.roll(high_edge, turn, 1)
        low = pltpu.roll(low_edge, turn, 1)
        inner = rows[pl.ds(g, devices, stride=2 * groups), :]
        outer = rows[pl.ds(groups + g, devices, stride=2 * groups), :]
        inner = inner + jnp.where(tail, high, jnp.where(head, low, 0.0))
        outer = jnp.where(keep, outer + jnp.where(head, high, low), 0.0)
        inner, outer = inner.astype(jnp.bfloat16), outer.astype(jnp.bfloat16)
        columns = slice(g * samples, (g + 1) * samples)
        for b in range(tap_count):
            move = b - reach
            if move > 0:
                both = jnp.where(lane < move, outer, inner)
            else:
                both = jnp.where(lane >= samples + move, outer, inner)
            turned = pltpu.roll(both, (-move) % samples, 1) if move else inner
            framed[b * devices : (b + 1) * devices, columns] = turned
        if g % 2 == 1 or g == groups - 1:
            columns = slice(g // 2 * 2 * samples, (g + 1) * samples)
            out_ref[:, columns] = jnp.dot(
                dip, framed[:, columns], preferred_element_type=jnp.float32
            ).astype(jnp.bfloat16)

    sent = send.at[pl.ds(0, devices - 1)]
    pltpu.make_async_copy(sent, sent, send_sem).wait()
    for there, slot in ((has_low, 0), (has_high, 1)):
        @pl.when(there)
        def _():
            pltpu.make_async_copy(pack.at[slot], pack.at[slot], pack_sem.at[slot]).wait()


def on_device(devices, records, fan_taps, dip_taps, live_mask, node_place, shot_place):
    _, comps, nodes, samples = records.shape
    each = nodes // devices
    groups = comps * each
    slots = fan_taps.shape[1] + 1
    taps = jnp.concatenate([fan_taps, dip_taps[None]])
    vmem = pl.BlockSpec(memory_space=pltpu.VMEM)
    result = pl.pallas_call(
        kernel,
        out_shape=jax.ShapeDtypeStruct((devices, groups * samples), jnp.bfloat16),
        in_specs=[vmem] * 5,
        out_specs=vmem,
        scratch_shapes=[
            pltpu.VMEM((comps, nodes, slots * nodes), jnp.bfloat16),
            pltpu.VMEM((comps, slots * nodes, 2 * samples), jnp.bfloat16),
            pltpu.VMEM((slots * devices, groups * samples), jnp.bfloat16),
            pltpu.VMEM((devices, 2 * groups, samples), jnp.bfloat16),
            pltpu.VMEM((devices, 2 * groups, samples), jnp.bfloat16),
            pltpu.VMEM((devices * 2 * groups, samples), jnp.float32),
            pltpu.VMEM((devices * 2 * groups, samples), jnp.float32),
            pltpu.VMEM((2, devices, 1, samples), jnp.float32),
            pltpu.VMEM((devices, 1, samples), jnp.float32),
            pltpu.VMEM((devices, 1, samples), jnp.float32),
            pltpu.SemaphoreType.DMA,
            pltpu.SemaphoreType.DMA,
            pltpu.SemaphoreType.DMA((2,)),
            pltpu.SemaphoreType.DMA,
            pltpu.SemaphoreType.DMA,
        ],
        compiler_params=pltpu.CompilerParams(
            collective_id=0, has_side_effects=True, vmem_limit_bytes=48 * 1024 * 1024
        ),
    )(records, taps, live_mask, node_place[None], shot_place[None])
    return result.reshape(devices, comps, each, samples)


def solution(mesh):
    return jax.shard_map(
        functools.partial(on_device, mesh.shape["shot"]),
        mesh=mesh,
        in_specs=(P("shot", None, None, "tm"), P(), P(), P("shot", None), P(), P()),
        out_specs=P(None, None, "shot", "tm"),
        check_vma=False,
    )
```
